512 devices in a mesh: seq: 64 (over z, x), kvh: 8 (over y, core).
Axes of the slice: x: 4, y: 4, z: 16, core: 2. Of those that a mesh axis runs over, the one named last changes fastest.
Arguments:
- hidden: bfloat16 [16, 8192], P(None, 'seq'), may hold values from -4 to 4
- filter_query: bfloat16 [16, 8192], P(None, 'kvh'), as said below
- new_entry: bfloat16 [16, 2048], P(None, 'kvh'), may hold values from -6 to 6
- filter_cache: bfloat16 [16, 8192, 2048], P(None, 'seq', 'kvh'), as said below
- out_weight: bfloat16 [8192, 8192], P('kvh', 'seq'), may hold values from -0.0625 to 0.0625
- next_gain: float32 [8192], P('seq'), may hold values from 0.5 to 2
- next_weight: bfloat16 [8192, 8, 1280], P('seq', 'kvh'), may hold values from -0.0625 to 0.0625
- next_cache: bfloat16 [16, 8192, 2048], P(None, 'seq', 'kvh'), as said below
- lengths: int32 [16], replicated, may hold values from 4096 to 8192, as said below
- selected: int32 [16, 2048], replicated, may hold values from 0 to 8191, as said below
Outputs:
- filter_out: bfloat16 [16, 8192], P(None, 'kvh')
- next_hidden: bfloat16 [16, 8192], P(None, 'seq')
- compact_cache: bfloat16 [64, 512, 2048], P('seq', None, 'kvh')
- select_out: bfloat16 [16, 8192], P(None, 'kvh')
The draws below stay inside these ranges and needn't reach their ends.
Inputs may be any that keep to these rules, and one draw needn't show every extreme that they name: The new token of request r stands at position lengths[r]; some request has exactly 8192. `selected`: each request's 2048 positions are distinct, ascending and below lengths[r]. For each request at most 64 of them lie in any aligned block of 128 positions, and in every draw some request has exactly 64 in one block. `filter_query`: rotated queries of order 2.5. `filter_cache`: cached keys and values of order one. `next_cache`: cached keys and values of order one.
All inputs are finite; a program needn't handle non-finite values.
Results may differ from the reference program's by a relative error of at most 0.038.
Values may be sent and summed in bfloat16 or wider, within the bound.
A program may use at most 64 MiB of HBM per device.

```python
import math
import jax
import jax.numpy as jnp
from jax import lax

D = 8192
HEADS = 64
KVH = 8
HD = 128
GROUP = 8
REQS = 16
REQUEST_CAPACITY = 8192
SEL = 2048
SHARD = 128
CAP = 64
OWN = 4
OSEL = 512


def pick_tokens(key):
    keys_all = jax.random.split(key, 4)
    longest_length = jax.random.randint(keys_all[0], (), 0, REQS)
    drawn = jax.random.randint(keys_all[1], (REQS,), REQUEST_CAPACITY // 2, REQUEST_CAPACITY + 1)
    request_ids = jnp.arange(REQS, dtype=jnp.int32)
    lengths = jnp.where(request_ids == longest_length, REQUEST_CAPACITY, drawn).astype(jnp.int32)
    mandatory_tokens = jax.random.randint(keys_all[2], (), 0, REQUEST_CAPACITY // 2 // SHARD)
    positions = jnp.arange(REQUEST_CAPACITY, dtype=jnp.int32)
    block_owner = positions // SHARD

    def one_request(request_key, length, request_number):
        first_key, second_key = jax.random.split(request_key)
        order_first = jax.random.permutation(first_key, REQUEST_CAPACITY).astype(jnp.int32).reshape(REQUEST_CAPACITY // SHARD, SHARD)
        ranks = jnp.argsort(jnp.argsort(order_first, axis=1), axis=1).reshape(REQUEST_CAPACITY)
        allowed_mask = (ranks < CAP) & (positions < length)
        secondary_order = jax.random.permutation(second_key, REQUEST_CAPACITY).astype(jnp.int32)
        extra_score = jnp.where((request_number == longest_length) & (block_owner == mandatory_tokens), REQUEST_CAPACITY, 0)
        selection_rank = jnp.where(allowed_mask, secondary_order + extra_score, -1).astype(jnp.int32)
        chosen = lax.top_k(selection_rank, SEL)[1]
        return jnp.sort(chosen.astype(jnp.int32))
    selected = jax.vmap(one_request)(jax.random.split(keys_all[3], REQS), lengths, request_ids)
    return (lengths, selected.astype(jnp.int32))


def draw_lengths(key, part):
    return pick_tokens(jax.random.fold_in(key, 7))[0]


def draw_selected(key, part):
    return pick_tokens(jax.random.fold_in(key, 7))[1]


def make_query(key):
    query_key = jax.random.fold_in(key, 13)
    values = jnp.clip(jax.random.normal(query_key, (REQS, HEADS * HD), jnp.float32), -6.0, 6.0) * 2.5
    return values


def draw_filter_query(key, part):
    return make_query(key).astype(jnp.bfloat16)


def drawn_cache(cache_key):
    key_first, key_second = jax.random.split(cache_key)
    values = jnp.clip(jax.random.normal(key_second, (REQS, REQUEST_CAPACITY, KVH, HD), jnp.float32), -6.0, 6.0)
    keys = jnp.clip(jax.random.normal(key_first, (REQS, REQUEST_CAPACITY, KVH, HD), jnp.float32), -6.0, 6.0)
    return (keys, values)


def pack_cache(keys, values):
    return jnp.stack([keys, values], axis=3).reshape(REQS, REQUEST_CAPACITY, KVH * 2 * HD).astype(jnp.bfloat16)


def draw_filter_cache(key, part):
    cache_key = jax.random.fold_in(key, 17)
    keys, values = drawn_cache(cache_key)
    return pack_cache(keys, values)


def draw_next_cache(key, part):
    cache_key = jax.random.fold_in(key, 19)
    keys, values = drawn_cache(cache_key)
    return pack_cache(keys, values)


def level_of(own_key, shape, shards, smallest, largest):
    factor_of, own = 1.0, jax.random.fold_in(own_key, 6)
    for position, blocks in shards:
        heights = jnp.exp(jax.random.uniform(jax.random.fold_in(own, position), (blocks,), jnp.float32, smallest / len(shards), largest / len(shards)))
        factor_of = factor_of * jnp.repeat(heights, shape[position] // blocks).reshape([-1 if axis == position else 1 for axis in range(len(shape))])
    return factor_of


def normal_values(rng, dims, width, limit, cuts=(), kind=jnp.bfloat16):
    result = jax.random.normal(rng, dims, jnp.float32) * width
    if len(cuts) > 0:
        result = level_of(rng, dims, cuts, -0.22, 0.18) * result
    return jnp.clip(result, min=-limit, max=limit).astype(kind)


def setup_inputs(seed: int = 0) -> dict:
    streams_of = jax.random.split(jax.random.key(seed), 11)
    hidden = normal_values(streams_of[0], (REQS, D), 0.25, 4.0, ((1, 64),))
    filter_query = draw_filter_query(jax.random.fold_in(streams_of[10], 71), 0)
    new_entry = normal_values(streams_of[2], (REQS, KVH * 2 * HD), 1.0, 6.0, ((1, 8),))
    filter_cache = draw_filter_cache(jax.random.fold_in(streams_of[10], 71), 0)
    out_weight = normal_values(streams_of[4], (HEADS * HD, D), (HEADS * HD) ** -0.5, 0.0625, ((0, 8), (1, 64)))
    next_gain = jnp.clip(jnp.exp(math.log(2.0) - 1.3862944 * jax.random.uniform(streams_of[5], (D,), jnp.float32) ** level_of(streams_of[5], (D,), ((0, 64),), -0.2, 0.2)), 0.5, 2.0)
    next_weight = normal_values(streams_of[6], (D, KVH, (GROUP + 2) * HD), D ** -0.5, 0.0625, ((0, 64), (1, 8)))
    next_cache = draw_next_cache(jax.random.fold_in(streams_of[10], 71), 0)
    lengths = draw_lengths(jax.random.fold_in(streams_of[10], 71), 0)
    selected = draw_selected(jax.random.fold_in(streams_of[10], 71), 0)
    return {"hidden": hidden, "filter_query": filter_query, "new_entry": new_entry, "filter_cache": filter_cache, "out_weight": out_weight, "next_gain": next_gain, "next_weight": next_weight, "next_cache": next_cache, "lengths": lengths, "selected": selected}


NEG_FILL = -1e+30
ROPE_BASE = 500000.0
EPSILON = 1e-05

def rotary(values, lengths):
    half_dim = values.shape[-1] // 2
    inverse = 1.0 / ROPE_BASE ** (jnp.arange(half_dim, dtype=jnp.float32) * 2.0 / values.shape[-1])
    angles = lengths.astype(jnp.float32)[:, None] * inverse[None, :]
    view_shape = (values.shape[0],) + (1,) * (values.ndim - 2) + (half_dim,)
    cosine = jnp.cos(angles).reshape(view_shape)
    sine_part = jnp.sin(angles).reshape(view_shape)
    first_half = values[..., :half_dim]
    second_half = values[..., half_dim:]
    return jnp.concatenate([first_half * cosine - second_half * sine_part, second_half * cosine + first_half * sine_part], axis=-1)

def split_rows(cache_rows):
    shaped = cache_rows.reshape(cache_rows.shape[0], KVH, 2, HD)
    return (shaped[:, :, 0], shaped[:, :, 1])

def attend_request(query, keys, values, alive, new_key, new_value):
    score_scale = 1.0 / math.sqrt(HD)
    query_wide = query.astype(jnp.float32)
    scores = jnp.einsum('hgd,nhd->hgn', query_wide, keys.astype(jnp.float32)) * score_scale
    scores = jnp.where(alive[None, None, :], scores, NEG_FILL)
    own_score = jnp.einsum('hgd,hd->hg', query_wide, new_key.astype(jnp.float32)) * score_scale
    new_peak = jnp.maximum(lax.optimization_barrier(jnp.max(scores, axis=-1)), own_score)
    weights = jnp.where(alive[None, None, :], jnp.exp(scores - new_peak[..., None]), 0.0)
    own_weight = jnp.exp(own_score - new_peak)
    weight_sum = lax.optimization_barrier(jnp.sum(weights, axis=-1)) + own_weight
    rounded = lax.optimization_barrier(weights.astype(jnp.bfloat16)).astype(jnp.float32)
    own_rounded = lax.optimization_barrier(own_weight.astype(jnp.bfloat16)).astype(jnp.float32)
    weighted = jnp.einsum('hgn,nhd->hgd', rounded, values.astype(jnp.float32))
    weighted = weighted + own_rounded[..., None] * new_value.astype(jnp.float32)[:, None, :]
    return (weighted / weight_sum[..., None]).astype(jnp.bfloat16).reshape(-1)

def reference(hidden, filter_query, new_entry, filter_cache, out_weight, next_gain, next_weight, next_cache, lengths, selected):
    per_group = HEADS // KVH
    positions = jnp.arange(REQUEST_CAPACITY, dtype=jnp.int32)
    request_ids = jnp.arange(REQS, dtype=jnp.int32)

    def filter_one(request):
        query = filter_query[request].reshape(KVH, per_group, HD)
        keys, values = split_rows(filter_cache[request])
        fresh = new_entry[request].reshape(KVH, 2, HD)
        alive = positions < lengths[request]
        return attend_request(query, keys, values, alive, fresh[:, 0], fresh[:, 1])
    filter_out = lax.map(filter_one, request_ids)
    mixed_out = jnp.dot(filter_out, out_weight, preferred_element_type=jnp.float32)
    next_hidden = (hidden.astype(jnp.float32) + mixed_out).astype(jnp.bfloat16)
    widened = next_hidden.astype(jnp.float32)
    mean_square = lax.optimization_barrier(jnp.mean(widened * widened, axis=1))
    scaled = (widened * next_gain[None, :]).astype(jnp.bfloat16)
    projected = jnp.dot(scaled, next_weight.reshape(D, -1), preferred_element_type=jnp.float32)
    projected = projected * lax.rsqrt(mean_square + EPSILON)[:, None]
    projected = projected.reshape(REQS, KVH, per_group + 2, HD)
    next_query = rotary(projected[:, :, :per_group], lengths).astype(jnp.bfloat16)
    next_key = rotary(projected[:, :, per_group], lengths).astype(jnp.bfloat16)
    next_value = projected[:, :, per_group + 1].astype(jnp.bfloat16)
    gathered = jax.vmap(lambda cache_rows, indices: jnp.take(cache_rows, indices, axis=0))(next_cache, selected)
    compact_cache = gathered.reshape(REQS, OSEL, OWN, -1).transpose(0, 2, 1, 3).reshape(REQS * OWN, OSEL, -1)
    every_row = jnp.arange(SEL, dtype=jnp.int32) >= 0

    def select_one(request):
        keys, values = split_rows(gathered[request])
        return attend_request(next_query[request], keys, values, every_row, next_key[request], next_value[request])
    select_out = lax.map(select_one, request_ids)
    return (filter_out, next_hidden, compact_cache, select_out)
```

```python
import functools
import math

import jax
import jax.numpy as jnp
import numpy as np
from jax import lax
from jax.experimental import pallas as pl
from jax.experimental.pallas import tpu as pltpu
from jax.sharding import PartitionSpec as P

D = 8192
HD = 128
SEL = 2048
REQS = 16
HEADS = 8
ROWS = 128
NEG_FILL = -1e30
ROPE_BASE = 500000.0
EPSILON = 1e-05
SCALE = 1.0 / math.sqrt(HD)
MESH = pl.DeviceIdType.MESH
FAR_FIRST = (8, 7, 9, 6, 10, 5, 11, 4, 12, 3, 13, 2, 14, 1, 15)
F32 = jnp.float32
BF16 = jnp.bfloat16
WINDOWS = (0, 16, 28, 44, 60)


def nt_dot(a, b):
    return lax.dot_general(a, b, (((1,), (1,)), ((), ())), preferred_element_type=F32)


def iota(shape, axis):
    return lax.broadcasted_iota(jnp.int32, shape, axis)


def wait_bytes(view, sem):
    pltpu.make_async_copy(view, view, sem).wait()


def step(
    hidden_h, fq_h, ne_h, fc_h, ow_h, gain_h, nw_h, nc_h, lens, sel_h, inv_h,
    fo_o, nh_o, cc_o, so_o,
    hidden, fq, ne, fc, ow, gain, nw, nc, sel, inv,
    qs, bs, br, onehot, comp,
    axs, axms, axr, axmr, azs, azms, azr, azmr, foxs, fox,
    ybs, ybr, cxs, cxr, czs, czr, cas, car, dxs, dxr, fins, fin,
    in_sem, s_sem, r_sem, m_sem, out_sem,
):
    seq = lax.axis_index("seq")
    kv = lax.axis_index("kvh")
    z, x = seq // 4, seq % 4
    base = seq * ROWS

    loads = {}
    for i, (name, src, dst) in enumerate((
        ("fq", fq_h, fq), ("fc", fc_h, fc), ("sel", sel_h, sel), ("nc", nc_h, nc), ("ne", ne_h, ne),
        ("ow", ow_h, ow), ("hidden", hidden_h, hidden), ("gain", gain_h, gain), ("nw", nw_h, nw), ("inv", inv_h, inv),
    )):
        loads[name] = pltpu.make_async_copy(src, dst, in_sem.at[i])
        loads[name].start()

    barrier = pltpu.get_barrier_semaphore()

    def greet(d, carry):
        pl.semaphore_signal(barrier, inc=1, device_id=((seq + d) % 64, kv), device_id_type=MESH)
        return carry

    lax.fori_loop(1, 64, greet, 0)
    for d in range(1, 8):
        pl.semaphore_signal(barrier, inc=1, device_id=(seq, (kv + d) % 8), device_id_type=MESH)

    def push(src, dst, sem, target):
        pltpu.make_async_remote_copy(
            src_ref=src, dst_ref=dst, send_sem=s_sem.at[sem], recv_sem=r_sem.at[sem],
            device_id=target, device_id_type=MESH,
        ).start()

    def x_peer(d):
        return (x + d) % 4

    def at_x(p):
        return (z * 4 + p, kv)

    def at_z(p):
        return (p * 4 + x, kv)

    loads["fq"].wait()
    loads["fc"].wait()
    for c in range(4):
        qs[c] = jnp.concatenate(
            [fq[:, (2 * c + i) * HD : (2 * c + i + 1) * HD] for i in range(2)], axis=0
        )
    query = qs[...].reshape(HEADS * REQS, HD)
    keys = fc[:, :, 0:HD].reshape(REQS * ROWS, HD)
    values = fc[:, :, HD : 2 * HD].reshape(REQS * ROWS, HD)
    lane1 = iota((1, ROWS), 1)
    row_req = iota((HEADS * REQS, ROWS), 0) % REQS
    scores = nt_dot(query, keys) * SCALE
    masked, alive = [], []
    for r in range(REQS):
        live = jnp.where((lane1 + base) < lens[r], r, -1)
        ok = row_req == live
        alive.append(ok)
        masked.append(jnp.where(ok, scores[:, r * ROWS : (r + 1) * ROWS], NEG_FILL))
    peak = masked[0]
    for r in range(1, REQS):
        peak = jnp.maximum(peak, masked[r])
    peak = jnp.max(peak, axis=1, keepdims=True)
    total = jnp.zeros((HEADS * REQS, ROWS), F32)
    weights = []
    for r in range(REQS):
        w = jnp.where(alive[r], jnp.exp(masked[r] - peak), 0.0)
        total = total + w
        weights.append(w.astype(BF16))
    total = jnp.sum(total, axis=1, keepdims=True)
    number = jnp.dot(jnp.concatenate(weights, axis=1), values, preferred_element_type=F32)
    axs[...] = number.astype(BF16).reshape(4, 32, HD)
    lane = iota((HEADS * REQS, HD), 1)
    sub = iota((HEADS * REQS, HD), 0) % 32
    spread = jnp.where(lane == sub, peak, 0.0) + jnp.where(lane == sub + 32, total, 0.0)
    axms[...] = jnp.sum(spread.reshape(4, 32, HD), axis=1, keepdims=True)

    loads["sel"].wait()
    loads["nc"].wait()
    below = jnp.zeros((REQS, 128), F32)
    upto = jnp.zeros((REQS, 128), F32)
    for c in range(SEL // 128):
        chunk = sel[:, c * 128 : (c + 1) * 128]
        below = below + jnp.where(chunk < base, 1.0, 0.0)
        upto = upto + jnp.where(chunk < base + ROWS, 1.0, 0.0)
    first = jnp.sum(below, axis=1, keepdims=True).astype(jnp.int32)
    last = jnp.sum(upto, axis=1, keepdims=True).astype(jnp.int32)
    chunk0 = first >> 7
    win = [jnp.zeros((REQS, 128), jnp.int32) for _ in range(2)]
    for c in range(SEL // 128):
        chunk = sel[:, c * 128 : (c + 1) * 128]
        win[0] = win[0] + jnp.where(chunk0 == c, chunk, 0)
        win[1] = win[1] + jnp.where(chunk0 == c - 1, chunk, 0)
    entry = jnp.concatenate(
        [chunk0 * 128 + iota((REQS, 128), 1), chunk0 * 128 + 128 + iota((REQS, 128), 1)], axis=1
    )
    usable = (entry >= first) & (entry < last)
    slot = jnp.where(usable, (entry & 3) * 16 + ((entry - first) >> 2), -1)
    place = jnp.where(usable, jnp.concatenate(win, axis=1) - base, -1)
    slot_id = iota((64, 256), 0)
    row_id = iota((ROWS, 256), 0)
    for r in range(REQS):
        hit = jnp.where(slot_id == slot[r : r + 1, :], 1.0, 0.0).astype(BF16)
        row = jnp.where(row_id == place[r : r + 1, :], 1.0, 0.0).astype(BF16)
        choose = nt_dot(hit, row).astype(BF16)
        packed = jnp.dot(choose, nc[r], preferred_element_type=F32)
        bs[4 * r : 4 * r + 4] = packed.astype(BF16).reshape(4, 16, 2 * HD)

    pl.semaphore_wait(barrier, 70)

    def rows_window(w):
        def send(i, carry):
            n = i // 4
            dz = jnp.where(n % 2 == 1, 8 - (n + 1) // 2, 8 + n // 2)
            t = ((z + dz) % 16) * 4 + (x + i) % 4
            push(bs.at[t], br.at[seq], 0, (t, kv))
            return carry

        lax.fori_loop(WINDOWS[w], WINDOWS[w + 1], send, 0)
        if w == len(WINDOWS) - 2:
            lax.fori_loop(61, 64, send, 0)

    for d in (2, 1, 3):
        p = x_peer(d)
        push(axs.at[p], axr.at[x], 1, at_x(p))
        push(axms.at[p], axmr.at[x], 2, at_x(p))
    axr[x] = axs[x]
    axmr[x] = axms[x]
    rows_window(0)
    mine = sel[pl.ds(z, 1), :]
    src_col = iota((64, SEL), 0)
    starts = jnp.sum(jnp.where(mine < src_col * ROWS, 1.0, 0.0), axis=1, keepdims=True)
    ends = jnp.sum(jnp.where(mine < (src_col + 1) * ROWS, 1.0, 0.0), axis=1, keepdims=True)
    own_lane = iota((64, 1024), 1) >> 4 == iota((64, 1024), 0)
    starts = jnp.sum(jnp.where(own_lane, starts, 0.0), axis=0, keepdims=True).astype(jnp.int32)
    ends = jnp.sum(jnp.where(own_lane, ends, 0.0), axis=0, keepdims=True).astype(jnp.int32)
    index = starts + ((x - starts) & 3) + 4 * (iota((1, 1024), 1) & 15)
    target_row = jnp.where(index < ends, index >> 2, -1)
    for c in range(4):
        onehot[c * 128 : (c + 1) * 128, :] = jnp.where(
            iota((128, 1024), 0) + c * 128 == target_row, 1.0, 0.0
        ).astype(BF16)

    def recv(view, sem):
        wait_bytes(view, r_sem.at[sem])

    def merge(count, part, stats):
        table = stats[...].reshape(count, HD).T
        peaks, sums = table[0:32], table[32:64]
        top = jnp.max(peaks, axis=1, keepdims=True)
        fade = jnp.exp(peaks - top)
        mass = jnp.sum(fade * sums, axis=1, keepdims=True)
        acc = fade[:, 0:1] * part[0].astype(F32)
        for s in range(1, count):
            acc = acc + fade[:, s : s + 1] * part[s].astype(F32)
        return top, mass, acc

    recv(axr.at[pl.ds(0, 3)], 1)
    recv(axmr.at[pl.ds(0, 3)], 2)
    top, mass, acc = merge(4, axr, axmr)
    azs[...] = acc.astype(BF16)
    lane = iota((32, HD), 1)
    sub = iota((32, HD), 0)
    spread = jnp.where(lane == sub, top, 0.0) + jnp.where(lane == sub + 32, mass, 0.0)
    azms[...] = jnp.sum(spread, axis=0, keepdims=True)

    for d in FAR_FIRST:
        p = (z + d) % 16
        push(azs, azr.at[z], 3, at_z(p))
        push(azms, azmr.at[z], 4, at_z(p))
    azr[z] = azs[...]
    azmr[z] = azms[...]
    rows_window(1)
    loads["ne"].wait()
    fresh_key = jnp.concatenate([ne[:, 0:HD]] * 2, axis=0).astype(F32)
    fresh_value = jnp.concatenate([ne[:, HD : 2 * HD]] * 2, axis=0).astype(F32)
    own = jnp.sum(qs[x].astype(F32) * fresh_key, axis=1, keepdims=True) * SCALE
    recv(azr.at[pl.ds(0, 15)], 3)
    recv(azmr.at[pl.ds(0, 15)], 4)

    def close(top, mass, acc, own, fresh_value):
        peak = jnp.maximum(top, own)
        fade = jnp.exp(top - peak)
        mine = jnp.exp(own - peak)
        acc = acc * fade + mine.astype(BF16).astype(F32) * fresh_value
        return (acc / (mass * fade + mine)).astype(BF16)

    top, mass, acc = merge(16, azr, azmr)
    foxs[...] = close(top, mass, acc, own, fresh_value)
    for d in (2, 1, 3):
        p = x_peer(d)
        push(foxs, fox.at[x], 5, at_x(p))
    fox[x] = foxs[...]
    rows_window(2)
    loads["ow"].wait()
    loads["hidden"].wait()
    loads["gain"].wait()
    loads["nw"].wait()
    loads["inv"].wait()
    recv(fox.at[pl.ds(0, 3)], 5)
    out_rows = jnp.concatenate(
        [fox[h // 2, (h % 2) * 16 : (h % 2) * 16 + 16] for h in range(HEADS)], axis=1
    )
    ybs[...] = jnp.dot(out_rows, ow[...], preferred_element_type=F32)
    for d in (4, 3, 5, 2, 6, 1, 7):
        push(ybs, ybr.at[kv], 6, (seq, (kv + d) % 8))
    ybr[kv] = ybs[...]
    fo_o[...] = out_rows
    recv(ybr.at[pl.ds(0, 7)], 6)
    mixed = ybr[0]
    for i in range(1, 8):
        mixed = mixed + ybr[i]
    next_hidden = (hidden[...].astype(F32) + mixed).astype(BF16)
    nh_o[...] = next_hidden
    wide = next_hidden.astype(F32)
    scaled = (wide * gain[...]).astype(BF16)
    squares = jnp.sum(wide * wide, axis=1, keepdims=True)
    projected = jnp.dot(scaled, nw[...], preferred_element_type=F32)
    for b in range(10):
        cxs[b // 3, b % 3] = projected[:, b * HD : (b + 1) * HD]
    cxs[3, 1] = jnp.broadcast_to(squares, (REQS, HD))
    cxs[3, 2] = jnp.zeros((REQS, HD), F32)
    for d in (2, 1, 3):
        p = x_peer(d)
        push(cxs.at[p], cxr.at[x], 7, at_x(p))
    cxr[x] = cxs[x]
    rows_window(3)
    recv(cxr.at[pl.ds(0, 3)], 7)
    summed = cxr[0] + cxr[1] + cxr[2] + cxr[3]
    czs[...] = summed.reshape(3, REQS, 1, HD)
    for d in FAR_FIRST:
        p = (z + d) % 16
        push(czs.at[:, p], czr.at[z], 8, at_z(p))
    czr[z] = czs[:, z]
    angle = lens[z].astype(F32) * inv[...]
    cosine = jnp.cos(angle)
    sine = jnp.where(iota((1, HD), 1) < HD // 2, -jnp.sin(angle), jnp.sin(angle))
    recv(czr.at[pl.ds(0, 15)], 8)
    summed = czr[0]
    for s in range(1, 16):
        summed = summed + czr[s]
    cas[...] = summed
    for d in (2, 1, 3):
        p = x_peer(d)
        push(cas, car.at[x], 9, at_x(p))
    car[x] = cas[...]
    recv(car.at[pl.ds(0, 3)], 9)
    br[seq] = bs[seq]
    recv(br.at[pl.ds(0, 63)], 0)
    arrived = br[...].reshape(1024, 2 * HD)
    comp[...] = jnp.dot(onehot[...], arrived, preferred_element_type=F32).astype(BF16)
    compact_out = pltpu.make_async_copy(comp, cc_o.at[0], out_sem.at[0])
    compact_out.start()
    mine = car[...].reshape(12, HD)
    norm = lax.rsqrt(mine[10:11] / D + EPSILON)
    mine = mine * norm
    turned = mine * cosine + pltpu.roll(mine, HD // 2, 1) * sine
    next_query = turned[0:8].astype(BF16)
    next_key = turned[8:9].astype(BF16).astype(F32)
    next_value = mine[9:10].astype(BF16).astype(F32)
    scores = nt_dot(next_query, comp[:, 0:HD]) * SCALE
    peak = jnp.max(scores, axis=1, keepdims=True)
    weights = jnp.exp(scores - peak)
    total = jnp.sum(weights, axis=1, keepdims=True)
    number = jnp.dot(weights.astype(BF16), comp[:, HD : 2 * HD], preferred_element_type=F32)
    dxs[0:8] = number
    dxs[8:16] = jnp.where(iota((8, HD), 1) < 64, peak, total)
    for d in (2, 1, 3):
        p = x_peer(d)
        push(dxs, dxr.at[x], 10, at_x(p))
    dxr[x] = dxs[...]
    own = jnp.sum(next_query.astype(F32) * next_key, axis=1, keepdims=True) * SCALE
    recv(dxr.at[pl.ds(0, 3)], 10)
    peaks = [dxr[s, 8:16, 0:1] for s in range(4)]
    top = jnp.maximum(jnp.maximum(peaks[0], peaks[1]), jnp.maximum(peaks[2], peaks[3]))
    mass = jnp.zeros((8, 1), F32)
    acc = jnp.zeros((8, HD), F32)
    for s in range(4):
        fade = jnp.exp(peaks[s] - top)
        mass = mass + fade * dxr[s, 8:16, 64:65]
        acc = acc + fade * dxr[s, 0:8]
    fins[...] = close(top, mass, acc, own, next_value).astype(F32)
    for d in FAR_FIRST:
        p = (z + d) % 16
        push(fins, fin.at[z], 11, at_z(p))
    fin[z] = fins[...]

    def sent(view, sem):
        wait_bytes(view, s_sem.at[sem])

    sent(br.at[pl.ds(0, 63)], 0)
    sent(axr.at[pl.ds(0, 3)], 1)
    sent(axmr.at[pl.ds(0, 3)], 2)
    sent(azr.at[pl.ds(0, 15)], 3)
    sent(azmr.at[pl.ds(0, 15)], 4)
    sent(fox.at[pl.ds(0, 3)], 5)
    sent(ybr.at[pl.ds(0, 7)], 6)
    sent(cxr.at[pl.ds(0, 3)], 7)
    sent(czr.at[pl.ds(0, 15)], 8)
    sent(car.at[pl.ds(0, 3)], 9)
    sent(dxr.at[pl.ds(0, 3)], 10)
    compact_out.wait()
    recv(fin.at[pl.ds(0, 15)], 11)
    for h in range(HEADS):
        so_o[:, h * HD : (h + 1) * HD] = fin[:, h, :].astype(BF16)
    sent(fin.at[pl.ds(0, 15)], 11)


def per_device(
    hidden, filter_query, new_entry, filter_cache, out_weight, next_gain, next_weight, next_cache,
    lengths, selected,
):
    rate = (1.0 / ROPE_BASE ** (np.arange(HD // 2) * 2.0 / HD)).astype(np.float32)
    inverse = jnp.asarray(np.concatenate([rate, rate])[None, :])
    hbm = pl.BlockSpec(memory_space=pl.ANY)
    vmem = pl.BlockSpec(memory_space=pltpu.VMEM)
    smem = pl.BlockSpec(memory_space=pltpu.SMEM)
    v = pltpu.VMEM
    return pl.pallas_call(
        step,
        out_shape=(
            jax.ShapeDtypeStruct((REQS, HEADS * HD), BF16),
            jax.ShapeDtypeStruct((REQS, HD), BF16),
            jax.ShapeDtypeStruct((1, 512, 2 * HD), BF16),
            jax.ShapeDtypeStruct((REQS, HEADS * HD), BF16),
        ),
        in_specs=[hbm] * 8 + [smem, hbm, hbm],
        out_specs=(vmem, vmem, hbm, vmem),
        scratch_shapes=[
            v((REQS, HD), BF16), v((REQS, HEADS * HD), BF16), v((REQS, 2 * HD), BF16),
            v((REQS, ROWS, 2 * HD), BF16), v((HEADS * HD, HD), BF16), v((1, HD), F32), v((HD, 10 * HD), BF16),
            v((REQS, ROWS, 2 * HD), BF16), v((REQS, SEL), jnp.int32), v((1, HD), F32),
            v((4, 32, HD), BF16), v((64, 16, 2 * HD), BF16), v((64, 16, 2 * HD), BF16),
            v((512, 1024), BF16), v((512, 2 * HD), BF16),
            v((4, 32, HD), BF16), v((4, 1, HD), F32), v((4, 32, HD), BF16), v((4, 1, HD), F32),
            v((32, HD), BF16), v((1, HD), F32), v((16, 32, HD), BF16), v((16, 1, HD), F32),
            v((32, HD), BF16), v((4, 32, HD), BF16),
            v((REQS, HD), F32), v((8, REQS, HD), F32),
            v((4, 3, REQS, HD), F32), v((4, 3, REQS, HD), F32),
            v((3, REQS, 1, HD), F32), v((16, 3, 1, HD), F32),
            v((3, 1, HD), F32), v((4, 3, 1, HD), F32),
            v((16, HD), F32), v((4, 16, HD), F32),
            v((8, HD), F32), v((16, 8, HD), F32),
            pltpu.SemaphoreType.DMA((10,)), pltpu.SemaphoreType.DMA((12,)), pltpu.SemaphoreType.DMA((12,)),
            pltpu.SemaphoreType.DMA((1,)), pltpu.SemaphoreType.DMA((1,)),
        ],
        compiler_params=pltpu.CompilerParams(
            collective_id=0, has_side_effects=True, vmem_limit_bytes=60 * 1024 * 1024
        ),
        name="decode_step",
    )(
        hidden, filter_query, new_entry, filter_cache, out_weight, next_gain.reshape(1, -1),
        next_weight.reshape(next_weight.shape[0], -1), next_cache, lengths, selected, inverse,
    )


def solution(mesh):
    in_specs = (
        P(None, "seq"),
        P(None, "kvh"),
        P(None, "kvh"),
        P(None, "seq", "kvh"),
        P("kvh", "seq"),
        P("seq"),
        P("seq", "kvh", None),
        P(None, "seq", "kvh"),
        P(),
        P(),
    )
    out_specs = (P(None, "kvh"), P(None, "seq"), P("seq", None, "kvh"), P(None, "kvh"))
    return jax.shard_map(
        per_device, mesh=mesh, in_specs=in_specs, out_specs=out_specs, check_vma=False
    )
```

```python
import functools
import math

import jax
import jax.numpy as jnp
import numpy as np
from jax import lax
from jax.experimental import pallas as pl
from jax.experimental.pallas import tpu as pltpu
from jax.sharding import PartitionSpec as P

D = 8192
HD = 128
SEL = 2048
REQS = 16
HEADS = 8
ROWS = 128
NEG_FILL = -1e30
ROPE_BASE = 500000.0
EPSILON = 1e-05
SCALE = 1.0 / math.sqrt(HD)
MESH = pl.DeviceIdType.MESH
FAR_FIRST = (8, 7, 9, 6, 10, 5, 11, 4, 12, 3, 13, 2, 14, 1, 15)
F32 = jnp.float32
BF16 = jnp.bfloat16
YT = BF16
WINDOWS = (0, 4, 32, 60, 60)


def nt_dot(a, b):
    return lax.dot_general(a, b, (((1,), (1,)), ((), ())), preferred_element_type=F32)


def iota(shape, axis):
    return lax.broadcasted_iota(jnp.int32, shape, axis)


def wait_bytes(view, sem):
    pltpu.make_async_copy(view, view, sem).wait()


def step(
    hidden_h, fq_h, ne_h, fc_h, ow_h, gain_h, nw_h, nc_h, lens, sel_h, inv_h,
    fo_o, nh_o, cc_o, so_o,
    hidden, fq, ne, fc, owx, gain, nw, nc, sel, inv,
    qs, bs, br, onehot, comp,
    axs, axms, axr, axmr, azs, azms, azr, azmr, foxs, fox,
    ybs, ybr, cxs, cxr, czs, czr, car, dxs, dxr, fins, fin,
    in_sem, s_sem, r_sem, m_sem, out_sem,
):
    seq = lax.axis_index("seq")
    kv = lax.axis_index("kvh")
    z, x = seq // 4, seq % 4
    base = seq * ROWS

    loads = {}
    for i, (name, src, dst) in enumerate((
        ("fq", fq_h, fq), ("fc", fc_h, fc), ("sel", sel_h, sel), ("nc", nc_h, nc), ("ne", ne_h, ne),
        ("ow", ow_h.at[pl.ds(pl.multiple_of(x * 256, 256), 256)], owx.at[x]), ("hidden", hidden_h, hidden), ("gain", gain_h, gain), ("nw", nw_h, nw), ("inv", inv_h, inv),
    )):
        loads[name] = pltpu.make_async_copy(src, dst, in_sem.at[i])
        loads[name].start()

    barrier = pltpu.get_barrier_semaphore()

    def greet(d, carry):
        pl.semaphore_signal(barrier, inc=1, device_id=((seq + d) % 64, kv), device_id_type=MESH)
        return carry

    lax.fori_loop(1, 64, greet, 0)

    def greet_heads(i, carry):
        pl.semaphore_signal(
            barrier, inc=1, device_id=(z * 4 + i % 4, (kv + 1 + i // 4) % 8), device_id_type=MESH
        )
        return carry

    lax.fori_loop(0, 28, greet_heads, 0)

    def push(src, dst, sem, target):
        pltpu.make_async_remote_copy(
            src_ref=src, dst_ref=dst, send_sem=s_sem.at[sem], recv_sem=r_sem.at[sem],
            device_id=target, device_id_type=MESH,
        ).start()

    def x_peer(d):
        return (x + d) % 4

    def at_x(p):
        return (z * 4 + p, kv)

    def at_z(p):
        return (p * 4 + x, kv)

    loads["fq"].wait()
    loads["fc"].wait()
    for c in range(4):
        qs[c] = jnp.concatenate(
            [fq[:, (2 * c + i) * HD : (2 * c + i + 1) * HD] for i in range(2)], axis=0
        )
    query = qs[...].reshape(HEADS * REQS, HD)
    keys = fc[:, :, 0:HD].reshape(REQS * ROWS, HD)
    values = fc[:, :, HD : 2 * HD].reshape(REQS * ROWS, HD)
    lane1 = iota((1, ROWS), 1)
    row_req = iota((HEADS * REQS, ROWS), 0) % REQS
    scores = nt_dot(query, keys) * SCALE
    masked, alive = [], []
    for r in range(REQS):
        live = jnp.where((lane1 + base) < lens[r], r, -1)
        ok = row_req == live
        alive.append(ok)
        masked.append(jnp.where(ok, scores[:, r * ROWS : (r + 1) * ROWS], NEG_FILL))
    peak = masked[0]
    for r in range(1, REQS):
        peak = jnp.maximum(peak, masked[r])
    peak = jnp.max(peak, axis=1, keepdims=True)
    total = jnp.zeros((HEADS * REQS, ROWS), F32)
    weights = []
    for r in range(REQS):
        w = jnp.where(alive[r], jnp.exp(masked[r] - peak), 0.0)
        total = total + w
        weights.append(w.astype(BF16))
    total = jnp.sum(total, axis=1, keepdims=True)
    number = jnp.dot(jnp.concatenate(weights, axis=1), values, preferred_element_type=F32)
    axs[...] = number.astype(BF16).reshape(4, 32, HD)
    lane = iota((HEADS * REQS, HD), 1)
    sub = iota((HEADS * REQS, HD), 0) % 32
    spread = jnp.where(lane == sub, peak, 0.0) + jnp.where(lane == sub + 32, total, 0.0)
    axms[...] = jnp.sum(spread.reshape(4, 32, HD), axis=1, keepdims=True)

    loads["sel"].wait()
    loads["nc"].wait()
    below = jnp.zeros((REQS, 128), F32)
    upto = jnp.zeros((REQS, 128), F32)
    for c in range(SEL // 128):
        chunk = sel[:, c * 128 : (c + 1) * 128]
        below = below + jnp.where(chunk < base, 1.0, 0.0)
        upto = upto + jnp.where(chunk < base + ROWS, 1.0, 0.0)
    first = jnp.sum(below, axis=1, keepdims=True).astype(jnp.int32)
    last = jnp.sum(upto, axis=1, keepdims=True).astype(jnp.int32)
    chunk0 = first >> 7
    win = [jnp.zeros((REQS, 128), jnp.int32) for _ in range(2)]
    for c in range(SEL // 128):
        chunk = sel[:, c * 128 : (c + 1) * 128]
        win[0] = win[0] + jnp.where(chunk0 == c, chunk, 0)
        win[1] = win[1] + jnp.where(chunk0 == c - 1, chunk, 0)
    entry = jnp.concatenate(
        [chunk0 * 128 + iota((REQS, 128), 1), chunk0 * 128 + 128 + iota((REQS, 128), 1)], axis=1
    )
    usable = (entry >= first) & (entry < last)
    slot = jnp.where(usable, (entry & 3) * 16 + ((entry - first) >> 2), -1)
    place = jnp.where(usable, jnp.concatenate(win, axis=1) - base, -1)
    slot_id = iota((64, 256), 0)
    row_id = iota((ROWS, 256), 0)
    for r in range(REQS):
        hit = jnp.where(slot_id == slot[r : r + 1, :], 1.0, 0.0).astype(BF16)
        row = jnp.where(row_id == place[r : r + 1, :], 1.0, 0.0).astype(BF16)
        choose = nt_dot(hit, row).astype(BF16)
        packed = jnp.dot(choose, nc[r], preferred_element_type=F32)
        bs[4 * r : 4 * r + 4] = packed.astype(BF16).reshape(4, 16, 2 * HD)

    pl.semaphore_wait(barrier, 91)

    def rows_window(w):
        def send(i, carry):
            n = i // 4
            dz = jnp.where(n % 2 == 1, 8 - (n + 1) // 2, 8 + n // 2)
            t = ((z + dz) % 16) * 4 + (x + i) % 4
            push(bs.at[t], br.at[seq], 0, (t, kv))
            return carry

        lax.fori_loop(WINDOWS[w], WINDOWS[w + 1], send, 0)
        if w == len(WINDOWS) - 2:
            lax.fori_loop(61, 64, send, 0)

    for d in (2, 1, 3):
        p = x_peer(d)
        push(axs.at[p], axr.at[x], 1, at_x(p))
        push(axms.at[p], axmr.at[x], 2, at_x(p))
    axr[x] = axs[x]
    axmr[x] = axms[x]
    for d in (2, 1, 3):
        p = x_peer(d)
        push(ow_h.at[pl.ds(pl.multiple_of(p * 256, 256), 256)], owx.at[x], 9, at_x(p))
    rows_window(0)
    mine = sel[pl.ds(z, 1), :]
    src_col = iota((64, SEL), 0)
    starts = jnp.sum(jnp.where(mine < src_col * ROWS, 1.0, 0.0), axis=1, keepdims=True)
    ends = jnp.sum(jnp.where(mine < (src_col + 1) * ROWS, 1.0, 0.0), axis=1, keepdims=True)
    own_lane = iota((64, 1024), 1) >> 4 == iota((64, 1024), 0)
    starts = jnp.sum(jnp.where(own_lane, starts, 0.0), axis=0, keepdims=True).astype(jnp.int32)
    ends = jnp.sum(jnp.where(own_lane, ends, 0.0), axis=0, keepdims=True).astype(jnp.int32)
    index = starts + ((x - starts) & 3) + 4 * (iota((1, 1024), 1) & 15)
    target_row = jnp.where(index < ends, index >> 2, -1)
    for c in range(4):
        onehot[c * 128 : (c + 1) * 128, :] = jnp.where(
            iota((128, 1024), 0) + c * 128 == target_row, 1.0, 0.0
        ).astype(BF16)

    def recv(view, sem):
        wait_bytes(view, r_sem.at[sem])

    def merge(count, part, stats):
        table = stats[...].reshape(count, HD).T
        peaks, sums = table[0:32], table[32:64]
        top = jnp.max(peaks, axis=1, keepdims=True)
        fade = jnp.exp(peaks - top)
        mass = jnp.sum(fade * sums, axis=1, keepdims=True)
        acc = fade[:, 0:1] * part[0].astype(F32)
        for s in range(1, count):
            acc = acc + fade[:, s : s + 1] * part[s].astype(F32)
        return top, mass, acc

    recv(axr.at[pl.ds(0, 3)], 1)
    recv(axmr.at[pl.ds(0, 3)], 2)
    top, mass, acc = merge(4, axr, axmr)
    azs[...] = acc.astype(BF16)
    lane = iota((32, HD), 1)
    sub = iota((32, HD), 0)
    spread = jnp.where(lane == sub, top, 0.0) + jnp.where(lane == sub + 32, mass, 0.0)
    azms[...] = jnp.sum(spread, axis=0, keepdims=True)

    for d in FAR_FIRST:
        p = (z + d) % 16
        push(azs, azr.at[z], 3, at_z(p))
        push(azms, azmr.at[z], 4, at_z(p))
    azr[z] = azs[...]
    azmr[z] = azms[...]
    rows_window(1)
    loads["ne"].wait()
    fresh_key = jnp.concatenate([ne[:, 0:HD]] * 2, axis=0).astype(F32)
    fresh_value = jnp.concatenate([ne[:, HD : 2 * HD]] * 2, axis=0).astype(F32)
    own = jnp.sum(qs[x].astype(F32) * fresh_key, axis=1, keepdims=True) * SCALE
    recv(azr.at[pl.ds(0, 15)], 3)
    recv(azmr.at[pl.ds(0, 15)], 4)

    def close(top, mass, acc, own, fresh_value):
        peak = jnp.maximum(top, own)
        fade = jnp.exp(top - peak)
        mine = jnp.exp(own - peak)
        acc = acc * fade + mine.astype(BF16).astype(F32) * fresh_value
        return (acc / (mass * fade + mine)).astype(BF16)

    top, mass, acc = merge(16, azr, azmr)
    heads = close(top, mass, acc, own, fresh_value)
    foxs[...] = heads
    loads["ow"].wait()
    recv(owx.at[pl.ds(0, 3)], 9)
    pair = jnp.concatenate([heads[0:16], heads[16:32]], axis=1)
    for p in range(4):
        ybs[p] = jnp.dot(pair, owx[p], preferred_element_type=F32).astype(YT)

    def to_columns(i, carry):
        p = (x + 3 - i % 4) % 4
        push(ybs.at[p], ybr.at[x * 8 + kv], 6, (z * 4 + p, (kv + 4 + i // 4) % 8))
        return carry

    lax.fori_loop(0, 16, to_columns, 0)
    lax.fori_loop(20, 32, to_columns, 0)
    lax.fori_loop(16, 19, to_columns, 0)
    ybr[x * 8 + kv] = ybs[x]
    for d in (2, 1, 3):
        p = x_peer(d)
        push(foxs, fox.at[x], 5, at_x(p))
    fox[x] = foxs[...]
    rows_window(2)
    loads["hidden"].wait()
    loads["gain"].wait()
    loads["nw"].wait()
    loads["inv"].wait()
    recv(ybr.at[pl.ds(0, 31)], 6)
    mixed = ybr[0].astype(F32)
    for i in range(1, 32):
        mixed = mixed + ybr[i].astype(F32)
    next_hidden = (hidden[...].astype(F32) + mixed).astype(BF16)
    nh_o[...] = next_hidden
    wide = next_hidden.astype(F32)
    scaled = (wide * gain[...]).astype(BF16)
    squares = jnp.sum(wide * wide, axis=1, keepdims=True)
    projected = jnp.dot(scaled, nw[...], preferred_element_type=F32)
    for b in range(10):
        cxs[b // 3, b % 3] = projected[:, b * HD : (b + 1) * HD]
    cxs[3, 1] = jnp.broadcast_to(squares, (REQS, HD))
    cxs[3, 2] = jnp.zeros((REQS, HD), F32)
    for d in (2, 1, 3):
        p = x_peer(d)
        push(cxs.at[p], cxr.at[x], 7, at_x(p))
    cxr[x] = cxs[x]
    rows_window(3)
    recv(fox.at[pl.ds(0, 3)], 5)
    for h in range(HEADS):
        fo_o[:, h * HD : (h + 1) * HD] = fox[h // 2, (h % 2) * 16 : (h % 2) * 16 + 16]
    recv(cxr.at[pl.ds(0, 3)], 7)
    summed = cxr[0] + cxr[1] + cxr[2] + cxr[3]
    czs[...] = summed.reshape(3, REQS, 1, HD)

    def to_owner(i, carry):
        n = i // 4
        dz = jnp.where(n % 2 == 1, 8 - (n + 1) // 2, 8 + n // 2)
        zt = (z + dz) % 16
        push(czs.at[:, zt], czr.at[seq], 8, (zt * 4 + (x + i) % 4, kv))
        return carry

    lax.fori_loop(0, 60, to_owner, 0)
    lax.fori_loop(61, 64, to_owner, 0)
    czr[seq] = czs[:, z]
    angle = lens[z].astype(F32) * inv[...]
    cosine = jnp.cos(angle)
    sine = jnp.where(iota((1, HD), 1) < HD // 2, -jnp.sin(angle), jnp.sin(angle))
    recv(czr.at[pl.ds(0, 63)], 8)
    for p in range(4):
        summed = czr[p]
        for s in range(1, 16):
            summed = summed + czr[4 * s + p]
        car[p] = summed
    br[seq] = bs[seq]
    recv(br.at[pl.ds(0, 63)], 0)
    arrived = br[...].reshape(1024, 2 * HD)
    comp[...] = jnp.dot(onehot[...], arrived, preferred_element_type=F32).astype(BF16)
    compact_out = pltpu.make_async_copy(comp, cc_o.at[0], out_sem.at[0])
    compact_out.start()
    mine = car[...].reshape(12, HD)
    norm = lax.rsqrt(mine[10:11] / D + EPSILON)
    mine = mine * norm
    turned = mine * cosine + pltpu.roll(mine, HD // 2, 1) * sine
    next_query = turned[0:8].astype(BF16)
    next_key = turned[8:9].astype(BF16).astype(F32)
    next_value = mine[9:10].astype(BF16).astype(F32)
    scores = nt_dot(next_query, comp[:, 0:HD]) * SCALE
    peak = jnp.max(scores, axis=1, keepdims=True)
    weights = jnp.exp(scores - peak)
    total = jnp.sum(weights, axis=1, keepdims=True)
    number = jnp.dot(weights.astype(BF16), comp[:, HD : 2 * HD], preferred_element_type=F32)
    dxs[0:8] = number
    dxs[8:16] = jnp.where(iota((8, HD), 1) < 64, peak, total)
    for d in (2, 1, 3):
        p = x_peer(d)
        push(dxs, dxr.at[x], 10, at_x(p))
    dxr[x] = dxs[...]
    own = jnp.sum(next_query.astype(F32) * next_key, axis=1, keepdims=True) * SCALE
    recv(dxr.at[pl.ds(0, 3)], 10)
    peaks = [dxr[s, 8:16, 0:1] for s in range(4)]
    top = jnp.maximum(jnp.maximum(peaks[0], peaks[1]), jnp.maximum(peaks[2], peaks[3]))
    mass = jnp.zeros((8, 1), F32)
    acc = jnp.zeros((8, HD), F32)
    for s in range(4):
        fade = jnp.exp(peaks[s] - top)
        mass = mass + fade * dxr[s, 8:16, 64:65]
        acc = acc + fade * dxr[s, 0:8]
    fins[...] = close(top, mass, acc, own, next_value).astype(F32)
    for d in FAR_FIRST:
        p = (z + d) % 16
        push(fins, fin.at[z], 11, at_z(p))
    fin[z] = fins[...]

    def sent(view, sem):
        wait_bytes(view, s_sem.at[sem])

    sent(br.at[pl.ds(0, 63)], 0)
    sent(axr.at[pl.ds(0, 3)], 1)
    sent(axmr.at[pl.ds(0, 3)], 2)
    sent(azr.at[pl.ds(0, 15)], 3)
    sent(azmr.at[pl.ds(0, 15)], 4)
    sent(fox.at[pl.ds(0, 3)], 5)
    sent(ybr.at[pl.ds(0, 31)], 6)
    sent(owx.at[pl.ds(0, 3)], 9)
    sent(cxr.at[pl.ds(0, 3)], 7)
    sent(czr.at[pl.ds(0, 63)], 8)
    sent(dxr.at[pl.ds(0, 3)], 10)
    compact_out.wait()
    recv(fin.at[pl.ds(0, 15)], 11)
    for h in range(HEADS):
        so_o[:, h * HD : (h + 1) * HD] = fin[:, h, :].astype(BF16)
    sent(fin.at[pl.ds(0, 15)], 11)


def settle(a, b, c, d, a_o, b_o, c_o, d_o):
    a_o[...] = a[...]
    b_o[...] = b[...]
    c_o[...] = c[...]
    d_o[...] = d[...]


def per_device(
    hidden, filter_query, new_entry, filter_cache, out_weight, next_gain, next_weight, next_cache,
    lengths, selected,
):
    rate = (1.0 / ROPE_BASE ** (np.arange(HD // 2) * 2.0 / HD)).astype(np.float32)
    inverse = jnp.asarray(np.concatenate([rate, rate])[None, :])
    hbm = pl.BlockSpec(memory_space=pl.ANY)
    vmem = pl.BlockSpec(memory_space=pltpu.VMEM)
    smem = pl.BlockSpec(memory_space=pltpu.SMEM)
    v = pltpu.VMEM
    results = pl.pallas_call(
        step,
        out_shape=(
            jax.ShapeDtypeStruct((REQS, HEADS * HD), BF16),
            jax.ShapeDtypeStruct((REQS, HD), BF16),
            jax.ShapeDtypeStruct((1, 512, 2 * HD), BF16),
            jax.ShapeDtypeStruct((REQS, HEADS * HD), BF16),
        ),
        in_specs=[hbm] * 8 + [smem, hbm, hbm],
        out_specs=(vmem, vmem, hbm, vmem),
        scratch_shapes=[
            v((REQS, HD), BF16), v((REQS, HEADS * HD), BF16), v((REQS, 2 * HD), BF16),
            v((REQS, ROWS, 2 * HD), BF16), v((4, 2 * HD, HD), BF16), v((1, HD), F32), v((HD, 10 * HD), BF16),
            v((REQS, ROWS, 2 * HD), BF16), v((REQS, SEL), jnp.int32), v((1, HD), F32),
            v((4, 32, HD), BF16), v((64, 16, 2 * HD), BF16), v((64, 16, 2 * HD), BF16),
            v((512, 1024), BF16), v((512, 2 * HD), BF16),
            v((4, 32, HD), BF16), v((4, 1, HD), F32), v((4, 32, HD), BF16), v((4, 1, HD), F32),
            v((32, HD), BF16), v((1, HD), F32), v((16, 32, HD), BF16), v((16, 1, HD), F32),
            v((32, HD), BF16), v((4, 32, HD), BF16),
            v((4, REQS, HD), YT), v((32, REQS, HD), YT),
            v((4, 3, REQS, HD), F32), v((4, 3, REQS, HD), F32),
            v((3, REQS, 1, HD), F32), v((64, 3, 1, HD), F32),
            v((4, 3, 1, HD), F32),
            v((16, HD), F32), v((4, 16, HD), F32),
            v((8, HD), F32), v((16, 8, HD), F32),
            pltpu.SemaphoreType.DMA((10,)), pltpu.SemaphoreType.DMA((12,)), pltpu.SemaphoreType.DMA((12,)),
            pltpu.SemaphoreType.DMA((1,)), pltpu.SemaphoreType.DMA((1,)),
        ],
        compiler_params=pltpu.CompilerParams(
            collective_id=0, has_side_effects=True, vmem_limit_bytes=60 * 1024 * 1024
        ),
        name="decode_step",
    )(
        hidden, filter_query, new_entry, filter_cache, out_weight, next_gain.reshape(1, -1),
        next_weight.reshape(next_weight.shape[0], -1), next_cache, lengths, selected, inverse,
    )
    return pl.pallas_call(
        settle,
        out_shape=tuple(jax.ShapeDtypeStruct(o.shape, o.dtype) for o in results),
        in_specs=[vmem] * 4,
        out_specs=(vmem,) * 4,
        name="settle",
    )(*results)


def solution(mesh):
    in_specs = (
        P(None, "seq"),
        P(None, "kvh"),
        P(None, "kvh"),
        P(None, "seq", "kvh"),
        P("kvh", "seq"),
        P("seq"),
        P("seq", "kvh", None),
        P(None, "seq", "kvh"),
        P(),
        P(),
    )
    out_specs = (P(None, "kvh"), P(None, "seq"), P("seq", None, "kvh"), P(None, "kvh"))
    return jax.shard_map(
        per_device, mesh=mesh, in_specs=in_specs, out_specs=out_specs, check_vma=False
    )
```
